128 devices in a mesh: row: 4 (over y), col: 8 (over x_lo, z), dep: 4 (over x_hi, core).
Axes of the slice: x: 4 (x_hi: 2, x_lo: 2; x = x_hi * 2 + x_lo), y: 4, z: 4, core: 2. Of those that a mesh axis runs over, the one named last changes fastest.
Arguments:
- inputs: bfloat16 [1280, 8192], P(('row', 'dep'), 'col'), may hold values from -6 to 6
- grad_out: bfloat16 [1280, 8192], P(('row', 'dep'), 'col'), may hold values from -6 to 6
- w_gate: bfloat16 [8192, 16384], P('col', ('row', 'dep')), may hold values from -0.0625 to 0.0625
- w_up: bfloat16 [8192, 16384], P('col', ('row', 'dep')), may hold values from -0.0625 to 0.0625
- w_down: bfloat16 [16384, 8192], P(('row', 'dep'), 'col'), may hold values from -0.046875 to 0.046875
Outputs:
- grad_in: bfloat16 [1280, 8192], P(('row', 'dep'), 'col')
- grad_gate: bfloat16 [8192, 16384], P('col', ('row', 'dep'))
- grad_up: bfloat16 [8192, 16384], P('col', ('row', 'dep'))
- grad_down: bfloat16 [16384, 8192], P(('row', 'dep'), 'col')
The draws below stay inside these ranges and needn't reach their ends.
All inputs are finite; a program needn't handle non-finite values.
Results may differ from the reference program's by a relative error of at most 0.015.
Values may be sent and summed in bfloat16 or wider, within the bound.
A program may use at most 128 MiB of HBM per device.

```python
import jax
import jax.numpy as jnp
from jax import lax

D = 8192
FF = 16384
TOKENS = 1280


def block_levels(key, extent, pieces, smallest, high):
    level = 1.0
    for position, shards_of in pieces:
        steps = jax.random.uniform(jax.random.fold_in(jax.random.fold_in(key, 6), position), (shards_of,), jnp.float32, smallest / len(pieces), high / len(pieces))
        level = level * jnp.repeat(jnp.exp(steps), extent[position] // shards_of).reshape((-1,) + (1,) * (len(extent) - 1 - position))
    return level


def scatter_about(rng, extent, deviation, most, pieces=(), dtype=jnp.bfloat16):
    array = jax.random.normal(rng, extent, jnp.float32) * deviation
    if len(pieces) > 0:
        array = block_levels(rng, extent, pieces, -0.22, 0.18) * array
    return jnp.clip(array, min=-most, max=most).astype(dtype)


def setup_inputs(seed: int = 0) -> dict:
    key_of = jax.random.split(jax.random.key(seed), 6)
    return {
        "inputs": scatter_about(key_of[0], (TOKENS, D), 1.0, 6.0, ((0, 16), (1, 8))),
        "grad_out": scatter_about(key_of[1], (TOKENS, D), 1.0, 6.0, ((0, 16), (1, 8))),
        "w_gate": scatter_about(key_of[2], (D, FF), D ** -0.5, 0.0625, ((0, 8), (1, 16))),
        "w_up": scatter_about(key_of[3], (D, FF), D ** -0.5, 0.0625, ((0, 8), (1, 16))),
        "w_down": scatter_about(key_of[4], (FF, D), FF ** -0.5, 0.046875, ((0, 16), (1, 8))),
    }


def contract_rows(left, right):
    return lax.dot_general(left, right, (((0,), (0,)), ((), ())), preferred_element_type=jnp.float32)


def reference(inputs, grad_out, w_gate, w_up, w_down):
    gate = jnp.dot(inputs, w_gate, preferred_element_type=jnp.float32)
    upper = jnp.dot(inputs, w_up, preferred_element_type=jnp.float32)
    sig = jax.nn.sigmoid(gate)
    silu = gate * sig
    hidden = (silu * upper).astype(jnp.bfloat16)
    dhidden = lax.dot_general(grad_out, w_down, (((1,), (1,)), ((), ())), preferred_element_type=jnp.float32).astype(jnp.bfloat16)
    dhf = dhidden.astype(jnp.float32)
    dgate = (dhf * upper * sig * (1.0 + gate * (1.0 - sig))).astype(jnp.bfloat16)
    dup = (dhf * silu).astype(jnp.bfloat16)
    grad_down = contract_rows(hidden, grad_out).astype(jnp.bfloat16)
    grad_gate = contract_rows(inputs, dgate).astype(jnp.bfloat16)
    grad_up = contract_rows(inputs, dup).astype(jnp.bfloat16)
    back = lax.dot_general(dgate, w_gate, (((1,), (1,)), ((), ())), preferred_element_type=jnp.float32)
    back = back + lax.dot_general(dup, w_up, (((1,), (1,)), ((), ())), preferred_element_type=jnp.float32)
    return back.astype(jnp.bfloat16), grad_gate, grad_up, grad_down
```

```python
import functools

import jax
import jax.numpy as jnp
from jax import lax
from jax.experimental import pallas as pl
from jax.experimental.pallas import tpu as pltpu
from jax.sharding import PartitionSpec as P

MESH = pl.DeviceIdType.MESH
BF = jnp.bfloat16
F32 = jnp.float32

ORDER = ((0, 0), (1, 0), (-1, 0), (2, 0), (2, 1), (1, 1), (-1, 1), (0, 1))
POS = {b: i for i, b in enumerate(ORDER)}
NB = len(ORDER)
HB = 80
RB = 2 * HB
HX = 64
HZ = RB - HX
W = 1024
TOKENS = NB * RB
EARLY = 960
LATE = TOKENS - EARLY
NSEM = 256


def nt(a, b):
    return lax.dot_general(a, b, (((1,), (1,)), ((), ())), preferred_element_type=F32)


def tn(a, b):
    return lax.dot_general(a, b, (((0,), (0,)), ((), ())), preferred_element_type=F32)


def nn(a, b):
    return lax.dot_general(a, b, (((1,), (0,)), ((), ())), preferred_element_type=F32)


def local_grads(gate, upper, dhidden):
    sig = jax.nn.sigmoid(gate)
    silu = gate * sig
    hidden = (silu * upper).astype(BF)
    dhf = dhidden.astype(BF).astype(F32)
    dgate = (dhf * upper * sig * (1.0 + gate * (1.0 - sig))).astype(BF)
    dup = (dhf * silu).astype(BF)
    return hidden, dgate, dup


def f32(v):
    return v.astype(F32)


def kernel(
    x_in, dy_in, wg_in, wu_in, wd_in,
    gin_out, part_out, xyt_out, gt_out,
    xy, wg, wu, wd, px, pz, rx1, rz1, rz2p, rz2m, ry1, ry2p, ry2m, rq, g,
    ds, rsib, rc, rd, ws, ssem, rsem, lsem,
):
    y = lax.axis_index("row")
    col = lax.axis_index("col")
    dep = lax.axis_index("dep")
    xl, z = col // 4, lax.rem(col, 4)
    xh, c = dep // 2, lax.rem(dep, 2)

    def zrel(d):
        return lax.rem(z + (d % 4), 4)

    def qrel(other, d):
        return (xl + other - 2 * other * xl) * 4 + zrel(d)

    target = {
        "z+": (y, qrel(0, 1), dep),
        "z-": (y, qrel(0, 3), dep),
        "xl": (y, qrel(1, 0), dep),
        "y+": (lax.rem(y + 1, 4), col, dep),
        "y-": (lax.rem(y + 3, 4), col, dep),
        "x2": (y, col, (1 - xh) * 2 + c),
        "co": (y, col, xh * 2 + 1 - c),
    }
    zdir = {1: "z+", -1: "z-"}
    copies = {}

    def send(name, src, dst, to):
        i = len(copies)
        copy = pltpu.make_async_remote_copy(
            src_ref=src, dst_ref=dst, send_sem=ssem.at[i], recv_sem=rsem.at[i],
            device_id=target[to], device_id_type=MESH,
        )
        copies[name] = copy
        copy.start()

    def got(name):
        copies[name].wait_recv()

    loads = {
        "wg": pltpu.make_async_copy(wg_in, wg, lsem.at[0]),
        "wu": pltpu.make_async_copy(wu_in, wu, lsem.at[1]),
        "wd": pltpu.make_async_copy(wd_in, wd, lsem.at[2]),
    }

    def rows80(block):
        return pl.ds(pl.multiple_of(POS[block] * RB + c * HB, 16), HB)

    own = rows80((0, 0))
    load_x = pltpu.make_async_copy(x_in, xy.at[0, own], lsem.at[3])
    load_y = pltpu.make_async_copy(dy_in, xy.at[1, own], lsem.at[4])
    load_x.start()
    load_y.start()
    for name in ("wg", "wu", "wd"):
        loads[name].start()

    barrier = pltpu.get_barrier_semaphore()
    for to in target:
        pl.semaphore_signal(barrier, inc=1, device_id=target[to], device_id_type=MESH)
    pl.semaphore_wait(barrier, len(target))
    load_x.wait()
    load_y.wait()

    def pass_on(name, here, there, to):
        send(name, xy.at[:, rows80(here)], xy.at[:, rows80(there)], to)

    def sibling(block):
        pass_on(("as", block), block, block, "co")

    sibling((0, 0))
    pass_on("ayp0", (0, 0), (-1, 0), "y+")
    pass_on("aym0", (0, 0), (1, 0), "y-")
    pass_on("ax2", (0, 0), (0, 1), "x2")

    def a_ring():
        got("ayp0")
        sibling((-1, 0))
        pass_on("ayp2", (-1, 0), (2, 0), "y+")
        got("aym0")
        sibling((1, 0))
        got("ax2")
        sibling((0, 1))
        pass_on("aym1", (0, 1), (1, 1), "y-")
        pass_on("ayp1", (0, 1), (-1, 1), "y+")

    def a_second():
        got("ayp2")
        sibling((2, 0))
        got("aym1")
        sibling((1, 1))
        pass_on("aym2", (1, 1), (2, 1), "y-")
        got("ayp1")
        sibling((-1, 1))

    def a_last():
        got("aym2")
        sibling((2, 1))

    def sgn(k):
        return 1 if k % 2 == 0 else -1

    def mm(k):
        got(("as", ORDER[k]))
        rows = pl.ds(k * RB, RB)

        def tile(n, carry):
            cols = pl.ds(pl.multiple_of(n * 256, 256), 256)
            xv = xy[0, rows, :]
            outs = (nn(xv, wg[:, cols]), nn(xv, wu[:, cols]), nt(xy[1, rows, :], wd[cols, :]))
            for m in range(3):
                r = outs[m].astype(BF)
                for j in range(2):
                    piece = r[:, j * 128 : (j + 1) * 128]
                    zz = lax.rem(n, 2) * 2 + j
                    px[k, n // 2, zz, m] = piece[:HX]
                    pz[k, zz, n // 2, m] = piece[HX:]
            return carry

        lax.fori_loop(0, 4, tile, 0)
        u = -sgn(k)
        send(("x1", k), px.at[k, 1 - xl], rx1.at[k], "xl")
        send(("y1", k), pz.at[k, zrel(2)], ry1.at[k], zdir[u])
        send(("y2m", k), pz.at[k, zrel(-u)], ry2m.at[k], zdir[-u])

    def r1(k):
        s = sgn(k)
        u = -s
        got(("y1", k))
        pz[k, zrel(u)] = (f32(pz[k, zrel(u)]) + f32(ry1[k])).astype(BF)
        send(("y2p", k), pz.at[k, zrel(u)], ry2p.at[k], zdir[u])
        got(("x1", k))
        for d in (2, -s):
            px[k, xl, zrel(d)] = (f32(px[k, xl, zrel(d)]) + f32(rx1[k, zrel(d)])).astype(BF)
        send(("z1", k), px.at[k, xl, zrel(2)], rz1.at[k], zdir[s])
        send(("z2m", k), px.at[k, xl, zrel(-s)], rz2m.at[k], zdir[-s])

    def r2(k):
        s = sgn(k)
        got(("z1", k))
        px[k, xl, zrel(s)] = (
            f32(px[k, xl, zrel(s)]) + f32(rx1[k, zrel(s)]) + f32(rz1[k])
        ).astype(BF)
        send(("z2p", k), px.at[k, xl, zrel(s)], rz2p.at[k], zdir[s])
        got(("y2p", k))
        got(("y2m", k))
        pz[k, z, 1 - xl] = (
            f32(pz[k, z, 1 - xl]) + f32(ry2p[k, 1 - xl]) + f32(ry2m[k, 1 - xl])
        ).astype(BF)
        send(("q", k), pz.at[k, z, 1 - xl], rq.at[k], "xl")

    def piece(k, half, q):
        start, size = (k * RB, HX) if half == 0 else (k * RB + HX, HZ)
        return g.at[q, :, pl.ds(start, size)]

    def give(name, k, half, q, to):
        send((name, k), piece(k, half, q), piece(k, half, q), to)

    def el(k):
        q = qrel(0, 0)
        got(("z2p", k))
        got(("z2m", k))
        t = f32(px[k, xl, z]) + f32(rx1[k, z]) + f32(rz2p[k]) + f32(rz2m[k])
        res = local_grads(t[0], t[1], t[2])
        for m in range(3):
            g[q, m, pl.ds(k * RB, HX)] = res[m]
        give("cx0", k, 0, q, "xl")
        give("cp0", k, 0, q, "z+")
        give("cm0", k, 0, q, "z-")
        got(("q", k))
        t = f32(pz[k, z, xl]) + f32(ry2p[k, xl]) + f32(ry2m[k, xl]) + f32(rq[k])
        res = local_grads(t[0], t[1], t[2])
        for m in range(3):
            g[q, m, pl.ds(k * RB + HX, HZ)] = res[m]
        give("cp1", k, 1, q, "z+")
        give("cm1", k, 1, q, "z-")
        give("cx1", k, 1, q, "xl")

    def f1(k):
        s = sgn(k)
        u = -s
        got(("cx0", k))
        give("cxp0", k, 0, qrel(1, 0), "z+")
        give("cxm0", k, 0, qrel(1, 0), "z-")
        got(("cp0", k))
        got(("cm0", k))
        give("cf0", k, 0, qrel(0, -s), zdir[s])
        got(("cp1", k))
        got(("cm1", k))
        give("cf1", k, 1, qrel(0, -u), zdir[u])
        give("cxa", k, 1, qrel(0, -1), "xl")
        give("cxb", k, 1, qrel(0, 1), "xl")

    def f2(k):
        s = sgn(k)
        got(("cxp0", k))
        got(("cxm0", k))
        give("cxf0", k, 0, qrel(1, -s), zdir[s])
        got(("cf1", k))
        give("cxc", k, 1, qrel(0, 2), "xl")

    def dd(k):
        for name in ("cf0", "cxf0", "cx1", "cxa", "cxb", "cxc"):
            got((name, k))
        rows = pl.ds(k * RB, RB)

        def tile(n, carry):
            cols = pl.ds(pl.multiple_of(n * 256, 256), 256)
            dgate = jnp.concatenate([g[q, 1, rows] for q in range(8)], axis=1)
            dup = jnp.concatenate([g[q, 2, rows] for q in range(8)], axis=1)
            ds[k, :, cols] = (nt(dgate, wg[cols, :]) + nt(dup, wu[cols, :])).astype(BF)
            return carry

        lax.fori_loop(0, 4, tile, 0)
        theirs = pl.ds(pl.multiple_of((1 - c) * HB, 16), HB)
        send(("sib", k), ds.at[k, theirs], rsib.at[k], "co")

    mine = pl.ds(pl.multiple_of(c * HB, 16), HB)

    def chip_sum(block):
        k = POS[block]
        got(("sib", k))
        return f32(ds[k, mine]) + f32(rsib[k])

    def forward(name, block, total, dst, to):
        k = POS[block]
        ds[k, mine] = total.astype(BF)
        send(name, ds.at[k, mine], dst, to)

    def d_two0():
        forward("c0", (2, 0), chip_sum((2, 0)), rc.at[0], "y+")

    def d_two1():
        forward("c1", (2, 1), chip_sum((2, 1)), rc.at[1], "y-")

    def d_near0():
        forward("rc", (-1, 0), chip_sum((-1, 0)), rd.at[1], "y-")
        total = chip_sum((1, 0))
        got("c0")
        forward("ra", (1, 0), total + f32(rc[0]), rd.at[0], "y+")

    def d_near1():
        forward("rb", (1, 1), chip_sum((1, 1)), rd.at[2], "y+")

    def d_near2():
        total = chip_sum((-1, 1))
        got("c1")
        forward("rd", (-1, 1), total + f32(rc[1]), rd.at[3], "y-")

    def d_other():
        total = chip_sum((0, 1))
        got("rb")
        got("rd")
        forward("re", (0, 1), total + f32(rd[2]) + f32(rd[3]), rd.at[4], "x2")

    def d_final():
        total = chip_sum((0, 0))
        got("ra")
        got("rc")
        total = total + f32(rd[0]) + f32(rd[1])
        got("re")
        gin_out[...] = (total + f32(rd[4])).astype(BF)

    early = pl.ds(0, EARLY)
    wcopies = []

    def wgrad(m, n):
        cols = pl.ds(n * 256, 256)
        pair = jnp.concatenate([g[2 * n, m, early], g[2 * n + 1, m, early]], axis=1)
        if m == 0:
            ws[m, cols, :] = tn(pair, xy[1, early, :]).astype(BF)
        else:
            ws[m, :, cols] = tn(xy[0, early, :], pair).astype(BF)

    def wout(m):
        copy = pltpu.make_async_copy(ws.at[m], part_out.at[m], lsem.at[5 + m])
        copy.start()
        wcopies.append(copy)

    def late_xy():
        copy = pltpu.make_async_copy(xy.at[:, pl.ds(EARLY, LATE)], xyt_out, lsem.at[8])
        copy.start()
        wcopies.append(copy)

    def late_g():
        copy = pltpu.make_async_copy(g.at[:, :, pl.ds(EARLY, LATE)], gt_out, lsem.at[9])
        copy.start()
        wcopies.append(copy)

    def mm_first():
        for name in ("wg", "wu", "wd"):
            loads[name].wait()
        mm(0)

    steps = {"m": mm, "r1": r1, "r2": r2, "e": el, "f1": f1, "f2": f2, "d": dd}
    for step in SCHEDULE:
        if step[0] == "w":
            wgrad(step[1], step[2])
        elif step[0] == "wo":
            wout(step[1])
        elif step[0] in steps and not (step[0] == "m" and step[1] == 0):
            steps[step[0]](step[1])
        else:
            {
                "m": mm_first, "a1": a_ring, "a2": a_second, "a3": a_last,
                "d20": d_two0, "d21": d_two1, "dn0": d_near0, "dn1": d_near1,
                "dn2": d_near2, "do": d_other, "df": d_final, "lx": late_xy, "lg": late_g,
            }[step[0]]()

    for copy in copies.values():
        copy.wait_send()
    for copy in wcopies:
        copy.wait()


def make_schedule():
    s = [("m", 0), ("a1",), ("m", 1), ("r1", 0), ("m", 2), ("a2",), ("r1", 1), ("r2", 0)]
    s += [("m", 3), ("r1", 2), ("r2", 1), ("e", 0), ("a3",)]
    s += [("m", 4), ("r1", 3), ("r2", 2), ("e", 1), ("f1", 0)]
    s += [("m", 5), ("r1", 4), ("r2", 3), ("e", 2), ("f1", 1), ("f2", 0)]
    s += [("m", 6), ("r1", 5), ("r2", 4), ("e", 3), ("f1", 2), ("f2", 1), ("d", 0)]
    s += [("m", 7), ("lx",), ("r1", 6), ("r2", 5), ("e", 4), ("f1", 3), ("f2", 2), ("d", 1)]
    s += [("r1", 7), ("r2", 6), ("e", 5), ("f1", 4), ("f2", 3), ("d", 2)]
    s += [("r2", 7), ("e", 6), ("f1", 5), ("f2", 4), ("d", 3)]
    s += [("e", 7), ("f1", 6), ("f2", 5), ("d20",), ("d", 4)]
    s += [("f1", 7), ("f2", 6), ("d21",), ("dn0",), ("d", 5)]
    s += [("w", 0, 0), ("w", 0, 1), ("w", 0, 2), ("w", 0, 3), ("wo", 0)]
    s += [("f2", 7), ("dn1",), ("d", 6)]
    s += [("w", 1, 0), ("w", 1, 1), ("w", 1, 2), ("w", 1, 3), ("wo", 1)]
    s += [("dn2",), ("d", 7), ("lg",)]
    s += [("w", 2, 0), ("w", 2, 1), ("do",), ("w", 2, 2), ("w", 2, 3), ("wo", 2), ("df",)]
    return s


SCHEDULE = make_schedule()


def finish(part, xyt, gt):
    def body(part, xt, yt, gta, gtd, gate_out, up_out, down_out):
        for m, out in ((1, gate_out), (2, up_out)):
            rhs = jnp.concatenate([gta[q, m] for q in range(8)], axis=1)
            out[...] = (f32(part[m]) + tn(xt[0], rhs)).astype(BF)
        lhs = jnp.concatenate([gtd[0, 0], gtd[1, 0]], axis=1)
        down_out[...] = (f32(part[0]) + tn(lhs, yt[0])).astype(BF)

    whole = jax.ShapeDtypeStruct((W, W), BF)
    tile = pl.BlockSpec((256, W), lambda i: (i, 0))
    return pl.pallas_call(
        body,
        name="finish_weight_grads",
        grid=(4,),
        out_shape=(whole, whole, whole),
        in_specs=[
            pl.BlockSpec((3, 256, W), lambda i: (0, i, 0)),
            pl.BlockSpec((1, LATE, 256), lambda i: (0, 0, i)),
            pl.BlockSpec((1, LATE, W), lambda i: (1, 0, 0)),
            pl.BlockSpec((8, 3, LATE, 128), lambda i: (0, 0, 0, 0)),
            pl.BlockSpec((2, 1, LATE, 128), lambda i: (i, 0, 0, 0)),
        ],
        out_specs=(tile, tile, tile),
        compiler_params=pltpu.CompilerParams(vmem_limit_bytes=40 * 2**20),
    )(part, xyt, xyt, gt, gt)


def exchange(inputs, grad_out, w_gate, w_up, w_down):
    def vmem(*shape, dtype=BF):
        return pltpu.VMEM(shape, dtype)

    scratch = [
        vmem(2, TOKENS, W), vmem(W, W), vmem(W, W), vmem(W, W),
        vmem(NB, 2, 4, 3, HX, 128), vmem(NB, 4, 2, 3, HZ, 128),
        vmem(NB, 4, 3, HX, 128),
        vmem(NB, 3, HX, 128), vmem(NB, 3, HX, 128), vmem(NB, 3, HX, 128),
        vmem(NB, 2, 3, HZ, 128), vmem(NB, 2, 3, HZ, 128), vmem(NB, 2, 3, HZ, 128),
        vmem(NB, 3, HZ, 128),
        vmem(8, 3, TOKENS, 128),
        vmem(NB, RB, W), vmem(NB, HB, W), vmem(2, HB, W), vmem(5, HB, W),
        vmem(3, W, W),
        pltpu.SemaphoreType.DMA((NSEM,)), pltpu.SemaphoreType.DMA((NSEM,)),
        pltpu.SemaphoreType.DMA((10,)),
    ]
    anywhere = pl.BlockSpec(memory_space=pl.ANY)
    return pl.pallas_call(
        kernel,
        name="exchange",
        out_shape=(
            jax.ShapeDtypeStruct((HB, W), BF),
            jax.ShapeDtypeStruct((3, W, W), BF),
            jax.ShapeDtypeStruct((2, LATE, W), BF),
            jax.ShapeDtypeStruct((8, 3, LATE, 128), BF),
        ),
        in_specs=[anywhere] * 5,
        out_specs=(pl.BlockSpec(memory_space=pltpu.VMEM), anywhere, anywhere, anywhere),
        scratch_shapes=scratch,
        compiler_params=pltpu.CompilerParams(
            collective_id=0, has_side_effects=True, vmem_limit_bytes=58 * 2**20
        ),
    )(inputs, grad_out, w_gate, w_up, w_down)


def shards(inputs, grad_out, w_gate, w_up, w_down):
    grad_in, part, xyt, gt = exchange(inputs, grad_out, w_gate, w_up, w_down)
    grad_gate, grad_up, grad_down = finish(part, xyt, gt)
    return grad_in, grad_gate, grad_up, grad_down


def solution(mesh):
    return jax.shard_map(
        shards,
        mesh=mesh,
        in_specs=(
            P(("row", "dep"), "col"),
            P(("row", "dep"), "col"),
            P("col", ("row", "dep")),
            P("col", ("row", "dep")),
            P(("row", "dep"), "col"),
        ),
        out_specs=(
            P(("row", "dep"), "col"),
            P("col", ("row", "dep")),
            P("col", ("row", "dep")),
            P(("row", "dep"), "col"),
        ),
        check_vma=False,
    )
```

```python
import functools

import jax
import jax.numpy as jnp
from jax import lax
from jax.experimental import pallas as pl
from jax.experimental.pallas import tpu as pltpu
from jax.sharding import PartitionSpec as P

MESH = pl.DeviceIdType.MESH
BF = jnp.bfloat16
F32 = jnp.float32

ORDER = ((1, 0), (0, 1), (1, 1), (2, 1), (2, 0), (-1, 1), (-1, 0), (0, 0))
POS = {b: i for i, b in enumerate(ORDER)}
NB = len(ORDER)
HB = 80
RB = 2 * HB
W = 1024
TOKENS = NB * RB
OWN_ROW = POS[(0, 0)] * RB
EARLY = 1024
LATE = TOKENS - EARLY
FIRST = 768
CHUNKS = (
    (7, 0, 80), (0, 0, 48), (0, 48, 112), (1, 0, 160), (2, 0, 160), (3, 0, 160), (4, 0, 160),
    (5, 0, 160), (6, 0, 64), (6, 64, 96), (7, 80, 80),
)
NC = len(CHUNKS)
FSTEPS = 2
EVMEM, FVMEM = 58, 60
NSEND = NC + 2
NRECV = 22 * NC + 31
LAST = {
    s: ("cf0", "cxf0", "cx1", "cxa", "cxb", "cxc") + o
    for s, o in ((1, ("cm0", "cxm0")), (-1, ("cp0", "cxp0")))
}
SPLIT = {160: 64, 128: 48, 112: 48, 96: 32, 80: 32, 64: 32, 48: 16, 32: 16}


def chunk_rows(k):
    block, start, rows = CHUNKS[k]
    return block * RB + start, rows


def chunk_split(k):
    rows = CHUNKS[k][2]
    return SPLIT[rows], rows - SPLIT[rows]


def nt(a, b):
    return lax.dot_general(a, b, (((1,), (1,)), ((), ())), preferred_element_type=F32)


def tn(a, b):
    return lax.dot_general(a, b, (((0,), (0,)), ((), ())), preferred_element_type=F32)


def nn(a, b):
    return lax.dot_general(a, b, (((1,), (0,)), ((), ())), preferred_element_type=F32)


def local_grads(gate, upper, dhidden):
    sig = jax.nn.sigmoid(gate)
    silu = gate * sig
    hidden = (silu * upper).astype(BF)
    dhf = dhidden.astype(BF).astype(F32)
    dgate = (dhf * upper * sig * (1.0 + gate * (1.0 - sig))).astype(BF)
    dup = (dhf * silu).astype(BF)
    return hidden, dgate, dup


def f32(v):
    return v.astype(F32)


def kernel(
    x_in, dy_in, wg_in, wu_in, wd_in,
    gin_out, part_out, xyt_out, gt_out,
    xy, wg, wu, wd, chunks, g, ds, rsib, rc, rd, ws, ssem, rsem, lsem,
):
    y = lax.axis_index("row")
    col = lax.axis_index("col")
    dep = lax.axis_index("dep")
    xl, z = col // 4, lax.rem(col, 4)
    xh, c = dep // 2, lax.rem(dep, 2)

    def zrel(d):
        return lax.rem(z + (d % 4), 4)

    def qrel(other, d):
        return (xl + other - 2 * other * xl) * 4 + zrel(d)

    target = {
        "z+": (y, qrel(0, 1), dep),
        "z-": (y, qrel(0, 3), dep),
        "xl": (y, qrel(1, 0), dep),
        "y+": (lax.rem(y + 1, 4), col, dep),
        "y-": (lax.rem(y + 3, 4), col, dep),
        "x2": (y, col, (1 - xh) * 2 + c),
        "co": (y, col, xh * 2 + 1 - c),
    }
    zdir = {1: "z+", -1: "z-"}
    copies = {}
    whole = set()

    groups = {}

    def send(name, src, dst, to, group):
        recv = len(copies)
        out = groups.setdefault(group, len(groups))
        copy = pltpu.make_async_remote_copy(
            src_ref=src, dst_ref=dst, send_sem=ssem.at[out], recv_sem=rsem.at[recv],
            device_id=target[to], device_id_type=MESH,
        )
        copies[name] = copy
        copy.start()

    def got(*names):
        for name in names:
            copies[name].wait_recv()

    def wait_bytes(like, sem):
        pltpu.make_async_copy(like, like, sem).wait()

    loads = [
        pltpu.make_async_copy(src, dst, lsem.at[i])
        for i, (src, dst) in enumerate((
            (x_in, xy.at[0, pl.ds(OWN_ROW, HB)]), (dy_in, xy.at[1, pl.ds(OWN_ROW, HB)]),
            (wg_in, wg), (wu_in, wu), (wd_in, wd),
        ))
    ]
    for load in loads:
        load.start()
    barrier = pltpu.get_barrier_semaphore()
    for to in target:
        pl.semaphore_signal(barrier, inc=1, device_id=target[to], device_id_type=MESH)

    def pass_on(name, here, there, to, first=0, count=HB):
        rows = [pl.ds(POS[block] * RB + first, count) for block in (here, there)]
        send(name, xy.at[:, rows[0]], xy.at[:, rows[1]], to, "a")

    def sibling(block):
        start = POS[block] * RB
        send(("as", block), xy.at[:, pl.ds(start, HB)], xy.at[:, pl.ds(start + HB, HB)], "co", "a")

    def own():
        for load in loads[:2]:
            load.wait()

    def weights():
        for load in loads[2:]:
            load.wait()

    def init():
        pl.semaphore_wait(barrier, len(target))
        sibling((0, 0))
        pass_on("aym0a", (0, 0), (1, 0), "y-", 0, 48)
        pass_on("aym0", (0, 0), (1, 0), "y-", 48, 32)
        pass_on("ayp0", (0, 0), (-1, 0), "y+")

    def a0():
        pass_on("ax2", (0, 0), (0, 1), "x2")

    def a1():
        got("ayp0")
        sibling((-1, 0))
        pass_on("ayp2", (-1, 0), (2, 0), "y+")

    def a2a():
        got("aym0a")

    def a2():
        got("aym0")
        sibling((1, 0))

    def a3():
        got("ax2")
        sibling((0, 1))
        pass_on("aym1", (0, 1), (1, 1), "y-")
        pass_on("ayp1", (0, 1), (-1, 1), "y+")

    def a4():
        got("ayp2")
        sibling((2, 0))

    def a5():
        got("aym1")
        sibling((1, 1))
        pass_on("aym2", (1, 1), (2, 1), "y-")

    def a6():
        got("ayp1")
        sibling((-1, 1))

    def a7():
        got("aym2")
        sibling((2, 1))

    def sgn(k):
        return 1 if k % 2 == 0 else -1

    def mc(k):
        block, first, count = CHUNKS[k]
        if first + count > HB and block not in whole:
            whole.add(block)
            got(("as", ORDER[block]))
        px, pz = chunks[k][:2]
        start, size = chunk_rows(k)
        rows = pl.ds(start, size)
        hx = chunk_split(k)[0]

        def tile(n, carry):
            cols = pl.ds(pl.multiple_of(n * 256, 256), 256)
            xv = xy[0, rows, :]
            outs = (nn(xv, wg[:, cols]), nn(xv, wu[:, cols]), nt(xy[1, rows, :], wd[cols, :]))
            for m in range(3):
                r = outs[m].astype(BF)
                for j in range(2):
                    piece = r[:, j * 128 : (j + 1) * 128]
                    zz = lax.rem(n, 2) * 2 + j
                    px[n // 2, zz, m] = piece[:hx]
                    pz[zz, n // 2, m] = piece[hx:]
            return carry

        lax.fori_loop(0, 4, tile, 0)

    def mm(k):
        px, pz, rx1, rz1, rz2p, rz2m, ry1, ry2p, ry2m, rq = chunks[k]
        u = -sgn(k)
        send(("y1", k), pz.at[zrel(2)], ry1, zdir[u], k)
        send(("y2m", k), pz.at[zrel(-u)], ry2m, zdir[-u], k)
        send(("x1", k), px.at[1 - xl], rx1, "xl", k)

    def r1a(k):
        px, pz, rx1, rz1, rz2p, rz2m, ry1, ry2p, ry2m, rq = chunks[k]
        u = -sgn(k)
        got(("y1", k))
        pz[zrel(u)] = (f32(pz[zrel(u)]) + f32(ry1[...])).astype(BF)
        send(("y2p", k), pz.at[zrel(u)], ry2p, zdir[u], k)

    def r1b(k):
        px, pz, rx1, rz1, rz2p, rz2m, ry1, ry2p, ry2m, rq = chunks[k]
        s = sgn(k)
        got(("x1", k))
        px[xl, zrel(2)] = (f32(px[xl, zrel(2)]) + f32(rx1[zrel(2)])).astype(BF)
        send(("z1", k), px.at[xl, zrel(2)], rz1, zdir[s], k)
        px[xl, zrel(-s)] = (f32(px[xl, zrel(-s)]) + f32(rx1[zrel(-s)])).astype(BF)
        send(("z2m", k), px.at[xl, zrel(-s)], rz2m, zdir[-s], k)

    def r2a(k):
        px, pz, rx1, rz1, rz2p, rz2m, ry1, ry2p, ry2m, rq = chunks[k]
        s = sgn(k)
        got(("z1", k))
        px[xl, zrel(s)] = (
            f32(px[xl, zrel(s)]) + f32(rx1[zrel(s)]) + f32(rz1[...])
        ).astype(BF)
        send(("z2p", k), px.at[xl, zrel(s)], rz2p, zdir[s], k)

    def r2b(k):
        px, pz, rx1, rz1, rz2p, rz2m, ry1, ry2p, ry2m, rq = chunks[k]
        got(("y2p", k), ("y2m", k))
        pz[z, 1 - xl] = (
            f32(pz[z, 1 - xl]) + f32(ry2p[1 - xl]) + f32(ry2m[1 - xl])
        ).astype(BF)
        send(("q", k), pz.at[z, 1 - xl], rq, "xl", k)

    def piece(k, half, q):
        start, _ = chunk_rows(k)
        hx, hz = chunk_split(k)
        return g.at[q, :, pl.ds(start, hx) if half == 0 else pl.ds(start + hx, hz)]

    def give(name, k, half, q, to):
        send((name, k), piece(k, half, q), piece(k, half, q), to, k)

    def ea(k):
        px, pz, rx1, rz1, rz2p, rz2m, ry1, ry2p, ry2m, rq = chunks[k]
        q = qrel(0, 0)
        got(("z2p", k), ("z2m", k))
        t = f32(px[xl, z]) + f32(rx1[z]) + f32(rz2p[...]) + f32(rz2m[...])
        res = local_grads(t[0], t[1], t[2])
        for m in range(3):
            g[q, m, pl.ds(chunk_rows(k)[0], chunk_split(k)[0])] = res[m]
        give("cp1", k, 0, q, "z+")
        give("cm1", k, 0, q, "z-")
        give("cx1", k, 0, q, "xl")

    def eb(k):
        px, pz, rx1, rz1, rz2p, rz2m, ry1, ry2p, ry2m, rq = chunks[k]
        q = qrel(0, 0)
        got(("q", k))
        t = f32(pz[z, xl]) + f32(ry2p[xl]) + f32(ry2m[xl]) + f32(rq[...])
        res = local_grads(t[0], t[1], t[2])
        hx, hz = chunk_split(k)
        for m in range(3):
            g[q, m, pl.ds(chunk_rows(k)[0] + hx, hz)] = res[m]
        give("cx0", k, 1, q, "xl")
        give("cp0", k, 1, q, "z+")
        give("cm0", k, 1, q, "z-")

    def f1a(k):
        got(("cx0", k))
        give("cxp0", k, 1, qrel(1, 0), "z+")
        give("cxm0", k, 1, qrel(1, 0), "z-")

    def f1b(k):
        s = sgn(k)
        got(("cp0" if s == 1 else "cm0", k))
        give("cf0", k, 1, qrel(0, -s), zdir[s])

    def f1c(k):
        u = -sgn(k)
        got(("cp1" if u == 1 else "cm1", k))
        give("cf1", k, 0, qrel(0, -u), zdir[u])
        give("cxa", k, 0, qrel(0, -u), "xl")

    def f1d(k):
        u = -sgn(k)
        got(("cm1" if u == 1 else "cp1", k))
        give("cxb", k, 0, qrel(0, u), "xl")

    def f2a(k):
        s = sgn(k)
        got(("cxp0" if s == 1 else "cxm0", k))
        give("cxf0", k, 1, qrel(1, -s), zdir[s])

    def f2b(k):
        got(("cf1", k))
        give("cxc", k, 0, qrel(0, 2), "xl")

    def gather_done(k):
        for name in LAST[sgn(k)]:
            got((name, k))

    def dd(block, start, size):
        rows = pl.ds(block * RB + start, size)

        def tile(n, carry):
            cols = pl.ds(pl.multiple_of(n * 256, 256), 256)
            dgate = jnp.concatenate([g[q, 1, rows] for q in range(8)], axis=1)
            dup = jnp.concatenate([g[q, 2, rows] for q in range(8)], axis=1)
            ds[block, pl.ds(start, size), cols] = (
                nt(dgate, wg[cols, :]) + nt(dup, wu[cols, :])
            ).astype(BF)
            return carry

        lax.fori_loop(0, 4, tile, 0)
        if start + size == RB:
            send(("sib", block), ds.at[block, pl.ds(HB, HB)], rsib.at[block], "co", "d")

    def chip_sum(block):
        k = POS[block]
        got(("sib", k))
        return f32(ds[k, pl.ds(0, HB)]) + f32(rsib[k])

    def forward(name, block, total, dst, to):
        rows = (POS[block], pl.ds(0, HB))
        ds[rows] = total.astype(BF)
        send(name, ds.at[rows], dst, to, "d")

    def d20():
        forward("c0", (2, 0), chip_sum((2, 0)), rc.at[0], "y+")

    def d21():
        forward("c1", (2, 1), chip_sum((2, 1)), rc.at[1], "y-")

    def dn0a():
        forward("rc", (-1, 0), chip_sum((-1, 0)), rd.at[1], "y-")

    def dn0b():
        total = chip_sum((1, 0))
        got("c0")
        forward("ra", (1, 0), total + f32(rc[0]), rd.at[0], "y+")

    def dn1():
        forward("rb", (1, 1), chip_sum((1, 1)), rd.at[2], "y+")

    def dn2():
        total = chip_sum((-1, 1))
        got("c1")
        forward("rd", (-1, 1), total + f32(rc[1]), rd.at[3], "y-")

    def d_other():
        total = chip_sum((0, 1))
        got("rb", "rd")
        forward("re", (0, 1), total + f32(rd[2]) + f32(rd[3]), rd.at[4], "x2")

    def d_final():
        total = chip_sum((0, 0))
        got("ra", "rc")
        total = total + f32(rd[0]) + f32(rd[1])
        got("re")
        gin_out[...] = (total + f32(rd[4])).astype(BF)

    wcopies = []
    finished = [0, 0, 0]

    def wtile(i, rows):
        m, n = i // 4, i % 4
        cols = pl.ds(n * 256, 256)
        pair = jnp.concatenate([g[2 * n, m, rows], g[2 * n + 1, m, rows]], axis=1)
        if m == 0:
            return (m, cols), tn(pair, xy[1, rows, :])
        return (m, slice(None), cols), tn(xy[0, rows, :], pair)

    def w1(i):
        at, value = wtile(i, pl.ds(0, FIRST))
        ws[at] = value.astype(BF)

    def w2(i):
        at, value = wtile(i, pl.ds(FIRST, EARLY - FIRST))
        ws[at] = (f32(ws[at]) + value).astype(BF)
        finished[i // 4] += 1
        if finished[i // 4] == 4:
            out(ws.at[i // 4], part_out.at[i // 4])

    def out(src, dst):
        copy = pltpu.make_async_copy(src, dst, lsem.at[5 + len(wcopies)])
        copy.start()
        wcopies.append(copy)

    def late_xy():
        out(xy.at[:, pl.ds(EARLY, LATE)], xyt_out)

    def late_g():
        out(g.at[:, :, pl.ds(EARLY, LATE)], gt_out)

    steps = {
        OWN: own, WTS: weights, INIT: init, A0: a0, A1: a1, A2: a2, A2A: a2a, A3: a3, A4: a4,
        A5: a5, A6: a6, A7: a7, MC: mc, M: mm, R1A: r1a, R1B: r1b, R2A: r2a, R2B: r2b,
        EA: ea, EB: eb, F1A: f1a, F1B: f1b, F1C: f1c, F1D: f1d, F2A: f2a, F2B: f2b,
        G: gather_done, D: dd, D20: d20, D21: d21, DN0A: dn0a, DN0B: dn0b, DN1: dn1,
        DN2: dn2, DX: d_other, DF: d_final, W1: w1, W2: w2, LX: late_xy, LG: late_g,
    }
    for step in SCHEDULE:
        steps[step[0]](*step[1:])

    wait_bytes(xy.at[:, pl.ds(0, 15 * HB)], ssem.at[groups["a"]])
    wait_bytes(xy.at[0, pl.ds(0, 15 * HB)], ssem.at[groups["d"]])
    for k in range(NC):
        wait_bytes(g.at[pl.ds(0, 7), :, pl.ds(0, 2 * CHUNKS[k][2])], ssem.at[groups[k]])
    for copy in wcopies:
        copy.wait()


(
    OWN, WTS, INIT, A0, A1, A2, A2A, A3, A4, A5, A6, A7, MC, M, R1A, R1B, R2A, R2B, EA, EB,
    F1A, F1B, F1C, F1D, F2A, F2B, G, D, D20, D21, DN0A, DN0B, DN1, DN2, DX, DF, W1, W2, LX, LG,
) = range(40)
SCHEDULE = (
    (OWN,), (INIT,), (A0,), (WTS,), (MC, 0), (M, 0), (R1A, 0), (A2A,), (MC, 1), (M, 1), (A2,),
    (A1,), (A3,), (R2B, 0), (MC, 2), (M, 2), (R1B, 0), (R1B, 1), (R1A, 1), (EB, 0), (MC, 3),
    (M, 3), (R1A, 2), (R2A, 0), (R2A, 1), (R1B, 2), (A4,), (R2B, 1), (A5,), (F1A, 0), (F1B, 0),
    (MC, 4), (M, 4), (R1B, 3), (EA, 0), (R1A, 3), (R2B, 2), (EA, 1), (F2A, 0), (R2A, 2), (EB, 1),
    (A6,), (A7,), (R1A, 4), (R1B, 4), (R2A, 3), (F1D, 0), (F1C, 0), (MC, 5), (F1A, 1), (M, 5),
    (F1D, 1), (R2B, 3), (F1C, 1), (F1B, 1), (EB, 2), (R2B, 4), (EA, 2), (R2A, 4), (EA, 3),
    (F2B, 0), (F2A, 1), (MC, 6), (M, 6), (R1B, 5), (F2B, 1), (R1A, 5), (F1B, 2), (EB, 3),
    (F1D, 2), (F1A, 2), (F1C, 2), (EA, 4), (F1D, 3), (F1C, 3), (EB, 4), (G, 0), (D, 7, 0, 80),
    (R1A, 6), (R2A, 5), (F1B, 3), (R1B, 6), (G, 1), (R2B, 5), (F2B, 2), (F1A, 3), (F1C, 4),
    (F2A, 2), (MC, 7), (F1D, 4), (M, 7), (F2B, 3), (R2B, 6), (F1B, 4), (EA, 5), (F1A, 4),
    (R2A, 6), (EB, 5), (G, 2), (D, 0, 0, 160), (F2A, 3), (F2B, 4), (MC, 8), (M, 8), (R1A, 7),
    (R1B, 7), (F1C, 5), (F1D, 5), (F2A, 4), (MC, 9), (M, 9), (EA, 6), (F1B, 5), (EB, 6), (G, 3),
    (F1A, 5), (D, 1, 0, 160), (R1A, 8), (R2A, 7), (R1B, 8), (R2B, 7), (F1C, 6), (F2B, 5),
    (R1B, 9), (G, 4), (D, 2, 0, 160), (R1A, 9), (F1A, 6), (F2A, 5), (MC, 10), (LX,), (M, 10),
    (EA, 7), (F1B, 6), (F1D, 6), (R2B, 8), (EB, 7), (F2B, 6), (DN1,), (R2A, 8), (R2A, 9),
    (R2B, 9), (R1B, 10), (G, 5), (D, 3, 0, 160), (F2A, 6), (R1A, 10), (EB, 8), (F1D, 7), (D21,),
    (F1C, 7), (F1A, 7), (F1B, 7), (EA, 9), (EB, 9), (F1A, 8), (R2B, 10), (EA, 8), (R2A, 10),
    (F2A, 7), (G, 6), (D, 4, 0, 160), (F2B, 7), (F1B, 8), (F1A, 9), (EB, 10), (F1B, 9), (F1D, 9),
    (D20,), (W1, 0), (W1, 2), (F1C, 8), (F1C, 9), (W1, 5), (W1, 6), (G, 7), (F2A, 8),
    (D, 5, 0, 160), (EA, 10), (F1D, 8), (F2A, 9), (F1A, 10), (W1, 7), (F1B, 10), (F2B, 8), (DN2,),
    (F2B, 9), (DN0B,), (W1, 9), (W1, 8), (W1, 1), (F1D, 10), (F1C, 10), (W1, 10), (F2A, 10),
    (W1, 11), (G, 8), (W2, 5), (G, 9), (D, 6, 0, 160), (F2B, 10), (W2, 0), (W2, 7), (W2, 2),
    (DX,), (W2, 1), (DN0A,), (W2, 6), (W2, 9), (W2, 8), (W2, 10), (W2, 11), (W1, 3), (G, 10),
    (LG,), (D, 7, 80, 80), (W2, 3), (W1, 4), (W2, 4), (DF,),
)


def finish(gin, part, xyt, gt):
    def body(gin, part, xt, yt, gta, gtd, gin_out, gate_out, up_out, down_out):
        gin_out[...] = gin[...]
        for m, out in ((1, gate_out), (2, up_out)):
            rhs = jnp.concatenate([gta[q, m] for q in range(8)], axis=1)
            out[...] = (f32(part[m]) + tn(xt[0], rhs)).astype(BF)
        lhs = jnp.concatenate([gtd[q, 0] for q in range(gtd.shape[0])], axis=1)
        down_out[...] = (f32(part[0]) + tn(lhs, yt[0])).astype(BF)

    whole = jax.ShapeDtypeStruct((W, W), BF)
    rows = W // FSTEPS
    tile = pl.BlockSpec((rows, W), lambda i: (i, 0))
    gin_tile = pl.BlockSpec((HB, W // FSTEPS), lambda i: (0, i))
    return pl.pallas_call(
        body,
        name="finish_weight_grads",
        grid=(FSTEPS,),
        out_shape=(jax.ShapeDtypeStruct((HB, W), BF), whole, whole, whole),
        in_specs=[
            gin_tile,
            pl.BlockSpec((3, rows, W), lambda i: (0, i, 0)),
            pl.BlockSpec((1, LATE, rows), lambda i: (0, 0, i)),
            pl.BlockSpec((1, LATE, W), lambda i: (1, 0, 0)),
            pl.BlockSpec((8, 3, LATE, 128), lambda i: (0, 0, 0, 0)),
            pl.BlockSpec((8 // FSTEPS, 1, LATE, 128), lambda i: (i, 0, 0, 0)),
        ],
        out_specs=(gin_tile, tile, tile, tile),
        compiler_params=pltpu.CompilerParams(vmem_limit_bytes=FVMEM * 2**20),
    )(gin, part, xyt, xyt, gt, gt)


def exchange(inputs, grad_out, w_gate, w_up, w_down):
    def vmem(*shape, dtype=BF):
        return pltpu.VMEM(shape, dtype)

    def chunk_scratch(k):
        hx, hz = chunk_split(k)
        return (
            vmem(2, 4, 3, hx, 128), vmem(4, 2, 3, hz, 128), vmem(4, 3, hx, 128),
            vmem(3, hx, 128), vmem(3, hx, 128), vmem(3, hx, 128),
            vmem(2, 3, hz, 128), vmem(2, 3, hz, 128), vmem(2, 3, hz, 128),
            vmem(3, hz, 128),
        )

    scratch = [
        vmem(2, TOKENS, W), vmem(W, W), vmem(W, W), vmem(W, W),
        [chunk_scratch(k) for k in range(NC)],
        vmem(8, 3, TOKENS, 128),
        vmem(NB, RB, W), vmem(NB, HB, W), vmem(2, HB, W), vmem(5, HB, W),
        vmem(3, W, W),
        pltpu.SemaphoreType.DMA((NSEND,)), pltpu.SemaphoreType.DMA((NRECV,)),
        pltpu.SemaphoreType.DMA((10,)),
    ]
    anywhere = pl.BlockSpec(memory_space=pl.ANY)
    return pl.pallas_call(
        kernel,
        name="exchange",
        out_shape=(
            jax.ShapeDtypeStruct((HB, W), BF),
            jax.ShapeDtypeStruct((3, W, W), BF),
            jax.ShapeDtypeStruct((2, LATE, W), BF),
            jax.ShapeDtypeStruct((8, 3, LATE, 128), BF),
        ),
        in_specs=[anywhere] * 5,
        out_specs=(pl.BlockSpec(memory_space=pltpu.VMEM), anywhere, anywhere, anywhere),
        scratch_shapes=scratch,
        compiler_params=pltpu.CompilerParams(
            collective_id=0, has_side_effects=True, vmem_limit_bytes=EVMEM * 2**20
        ),
    )(inputs, grad_out, w_gate, w_up, w_down)


def shards(inputs, grad_out, w_gate, w_up, w_down):
    grad_in, part, xyt, gt = exchange(inputs, grad_out, w_gate, w_up, w_down)
    return finish(grad_in, part, xyt, gt)


def solution(mesh):
    return jax.shard_map(
        shards,
        mesh=mesh,
        in_specs=(
            P(("row", "dep"), "col"),
            P(("row", "dep"), "col"),
            P("col", ("row", "dep")),
            P("col", ("row", "dep")),
            P(("row", "dep"), "col"),
        ),
        out_specs=(
            P(("row", "dep"), "col"),
            P("col", ("row", "dep")),
            P("col", ("row", "dep")),
            P(("row", "dep"), "col"),
        ),
        check_vma=False,
    )
```

```python
import functools

import jax
import jax.numpy as jnp
from jax import lax
from jax.experimental import pallas as pl
from jax.experimental.pallas import tpu as pltpu
from jax.sharding import PartitionSpec as P

MESH = pl.DeviceIdType.MESH
BF = jnp.bfloat16
F32 = jnp.float32

ORDER = ((1, 0), (0, 1), (2, 0), (2, 1), (1, 1), (-1, 1), (-1, 0), (0, 0))
POS = {b: i for i, b in enumerate(ORDER)}
NB = len(ORDER)
HB = 80
RB = 2 * HB
W = 1024
TOKENS = NB * RB
OWN_ROW = POS[(0, 0)] * RB
EARLY = 1024
LATE = TOKENS - EARLY
FIRST = 512
CHUNKS = (
    (7, 0, 80), (0, 0, 48), (0, 48, 112), (1, 0, 160), (2, 0, 160), (3, 0, 160), (4, 0, 160),
    (5, 0, 160), (6, 0, 64), (6, 64, 96), (7, 80, 80),
)
NC = len(CHUNKS)
FSTEPS = 2
EVMEM, FVMEM = 58, 60
NSEND = NC + 2
NRECV = 22 * NC + 31
LAST = {
    s: ("cf0", "cxf0", "cx1", "cxa", "cxb", "cxc") + o
    for s, o in ((1, ("cm0", "cxm0")), (-1, ("cp0", "cxp0")))
}
SPLIT = {160: 64, 128: 48, 112: 48, 96: 32, 80: 32, 64: 32, 48: 16, 32: 16}


def chunk_rows(k):
    block, start, rows = CHUNKS[k]
    return block * RB + start, rows


def chunk_split(k):
    rows = CHUNKS[k][2]
    return SPLIT[rows], rows - SPLIT[rows]


def nt(a, b):
    return lax.dot_general(a, b, (((1,), (1,)), ((), ())), preferred_element_type=F32)


def tn(a, b):
    return lax.dot_general(a, b, (((0,), (0,)), ((), ())), preferred_element_type=F32)


def nn(a, b):
    return lax.dot_general(a, b, (((1,), (0,)), ((), ())), preferred_element_type=F32)


def local_grads(gate, upper, dhidden):
    sig = jax.nn.sigmoid(gate)
    silu = gate * sig
    hidden = (silu * upper).astype(BF)
    dhf = dhidden.astype(BF).astype(F32)
    dgate = (dhf * upper * sig * (1.0 + gate * (1.0 - sig))).astype(BF)
    dup = (dhf * silu).astype(BF)
    return hidden, dgate, dup


def f32(v):
    return v.astype(F32)


def kernel(
    x_in, dy_in, wg_in, wu_in, wd_in,
    gin_out, part_out, xyt_out, gt_out,
    xy, wg, wu, wd, chunks, g, ds, rsib, rc, rd, ws, ssem, rsem, lsem,
):
    y = lax.axis_index("row")
    col = lax.axis_index("col")
    dep = lax.axis_index("dep")
    xl, z = col // 4, lax.rem(col, 4)
    xh, c = dep // 2, lax.rem(dep, 2)

    def zrel(d):
        return lax.rem(z + (d % 4), 4)

    def qrel(other, d):
        return (xl + other - 2 * other * xl) * 4 + zrel(d)

    target = {
        "z+": (y, qrel(0, 1), dep),
        "z-": (y, qrel(0, 3), dep),
        "xl": (y, qrel(1, 0), dep),
        "y+": (lax.rem(y + 1, 4), col, dep),
        "y-": (lax.rem(y + 3, 4), col, dep),
        "x2": (y, col, (1 - xh) * 2 + c),
        "co": (y, col, xh * 2 + 1 - c),
    }
    zdir = {1: "z+", -1: "z-"}
    copies = {}
    whole = set()

    groups = {}

    def send(name, src, dst, to, group):
        recv = len(copies)
        out = groups.setdefault(group, len(groups))
        copy = pltpu.make_async_remote_copy(
            src_ref=src, dst_ref=dst, send_sem=ssem.at[out], recv_sem=rsem.at[recv],
            device_id=target[to], device_id_type=MESH,
        )
        copies[name] = copy
        copy.start()

    def got(*names):
        for name in names:
            copies[name].wait_recv()

    def wait_bytes(like, sem):
        pltpu.make_async_copy(like, like, sem).wait()

    loads = [
        pltpu.make_async_copy(src, dst, lsem.at[i])
        for i, (src, dst) in enumerate((
            (x_in, xy.at[0, pl.ds(OWN_ROW, HB)]), (dy_in, xy.at[1, pl.ds(OWN_ROW, HB)]),
            (wg_in, wg), (wu_in, wu), (wd_in, wd),
        ))
    ]
    for load in loads:
        load.start()
    barrier = pltpu.get_barrier_semaphore()
    for to in target:
        pl.semaphore_signal(barrier, inc=1, device_id=target[to], device_id_type=MESH)

    def pass_on(name, here, there, to, first=0, count=HB):
        rows = [pl.ds(POS[block] * RB + first, count) for block in (here, there)]
        send(name, xy.at[:, rows[0]], xy.at[:, rows[1]], to, "a")

    def sibling(block):
        start = POS[block] * RB
        send(("as", block), xy.at[:, pl.ds(start, HB)], xy.at[:, pl.ds(start + HB, HB)], "co", "a")

    def own():
        for load in loads[:2]:
            load.wait()

    def weights():
        for load in loads[2:]:
            load.wait()

    def init():
        pl.semaphore_wait(barrier, len(target))
        sibling((0, 0))
        pass_on("aym0a", (0, 0), (1, 0), "y-", 0, 48)
        pass_on("aym0", (0, 0), (1, 0), "y-", 48, 32)
        pass_on("ayp0", (0, 0), (-1, 0), "y+")

    def a0():
        pass_on("ax2", (0, 0), (0, 1), "x2")

    def a1():
        got("ayp0")
        sibling((-1, 0))
        pass_on("ayp2", (-1, 0), (2, 0), "y+")

    def a2a():
        got("aym0a")

    def a2():
        got("aym0")
        sibling((1, 0))

    def a3():
        got("ax2")
        sibling((0, 1))
        pass_on("aym1", (0, 1), (1, 1), "y-")
        pass_on("ayp1", (0, 1), (-1, 1), "y+")

    def a4():
        got("ayp2")
        sibling((2, 0))

    def a5():
        got("aym1")
        sibling((1, 1))
        pass_on("aym2", (1, 1), (2, 1), "y-")

    def a6():
        got("ayp1")
        sibling((-1, 1))

    def a7():
        got("aym2")
        sibling((2, 1))

    def sgn(k):
        return 1 if k % 2 == 0 else -1

    def mc(k):
        block, first, count = CHUNKS[k]
        if first + count > HB and block not in whole:
            whole.add(block)
            got(("as", ORDER[block]))
        px, pz = chunks[k][:2]
        start, size = chunk_rows(k)
        rows = pl.ds(start, size)
        hx = chunk_split(k)[0]

        def tile(n, carry):
            cols = pl.ds(pl.multiple_of(n * 256, 256), 256)
            xv = xy[0, rows, :]
            outs = (nn(xv, wg[:, cols]), nn(xv, wu[:, cols]), nt(xy[1, rows, :], wd[cols, :]))
            for m in range(3):
                r = outs[m].astype(BF)
                for j in range(2):
                    piece = r[:, j * 128 : (j + 1) * 128]
                    zz = lax.rem(n, 2) * 2 + j
                    px[n // 2, zz, m] = piece[:hx]
                    pz[zz, n // 2, m] = piece[hx:]
            return carry

        lax.fori_loop(0, 4, tile, 0)

    def mm(k):
        px, pz, rx1, rz1, rz2p, rz2m, ry1, ry2p, ry2m, rq = chunks[k]
        u = -sgn(k)
        send(("y1", k), pz.at[zrel(2)], ry1, zdir[u], k)
        send(("y2m", k), pz.at[zrel(-u)], ry2m, zdir[-u], k)
        send(("x1", k), px.at[1 - xl], rx1, "xl", k)

    def r1a(k):
        px, pz, rx1, rz1, rz2p, rz2m, ry1, ry2p, ry2m, rq = chunks[k]
        u = -sgn(k)
        got(("y1", k))
        pz[zrel(u)] = (f32(pz[zrel(u)]) + f32(ry1[...])).astype(BF)
        send(("y2p", k), pz.at[zrel(u)], ry2p, zdir[u], k)

    def r1b(k):
        px, pz, rx1, rz1, rz2p, rz2m, ry1, ry2p, ry2m, rq = chunks[k]
        s = sgn(k)
        got(("x1", k))
        px[xl, zrel(2)] = (f32(px[xl, zrel(2)]) + f32(rx1[zrel(2)])).astype(BF)
        send(("z1", k), px.at[xl, zrel(2)], rz1, zdir[s], k)
        px[xl, zrel(-s)] = (f32(px[xl, zrel(-s)]) + f32(rx1[zrel(-s)])).astype(BF)
        send(("z2m", k), px.at[xl, zrel(-s)], rz2m, zdir[-s], k)

    def r2a(k):
        px, pz, rx1, rz1, rz2p, rz2m, ry1, ry2p, ry2m, rq = chunks[k]
        s = sgn(k)
        got(("z1", k))
        px[xl, zrel(s)] = (
            f32(px[xl, zrel(s)]) + f32(rx1[zrel(s)]) + f32(rz1[...])
        ).astype(BF)
        send(("z2p", k), px.at[xl, zrel(s)], rz2p, zdir[s], k)

    def r2b(k):
        px, pz, rx1, rz1, rz2p, rz2m, ry1, ry2p, ry2m, rq = chunks[k]
        got(("y2p", k), ("y2m", k))
        pz[z, 1 - xl] = (
            f32(pz[z, 1 - xl]) + f32(ry2p[1 - xl]) + f32(ry2m[1 - xl])
        ).astype(BF)
        send(("q", k), pz.at[z, 1 - xl], rq, "xl", k)

    def piece(k, half, q):
        start, _ = chunk_rows(k)
        hx, hz = chunk_split(k)
        return g.at[q, :, pl.ds(start, hx) if half == 0 else pl.ds(start + hx, hz)]

    def give(name, k, half, q, to):
        send((name, k), piece(k, half, q), piece(k, half, q), to, k)

    def ea(k):
        px, pz, rx1, rz1, rz2p, rz2m, ry1, ry2p, ry2m, rq = chunks[k]
        q = qrel(0, 0)
        got(("z2p", k), ("z2m", k))
        t = f32(px[xl, z]) + f32(rx1[z]) + f32(rz2p[...]) + f32(rz2m[...])
        res = local_grads(t[0], t[1], t[2])
        for m in range(3):
            g[q, m, pl.ds(chunk_rows(k)[0], chunk_split(k)[0])] = res[m]
        give("cp1", k, 0, q, "z+")
        give("cm1", k, 0, q, "z-")
        give("cx1", k, 0, q, "xl")

    def eb(k):
        px, pz, rx1, rz1, rz2p, rz2m, ry1, ry2p, ry2m, rq = chunks[k]
        q = qrel(0, 0)
        got(("q", k))
        t = f32(pz[z, xl]) + f32(ry2p[xl]) + f32(ry2m[xl]) + f32(rq[...])
        res = local_grads(t[0], t[1], t[2])
        hx, hz = chunk_split(k)
        for m in range(3):
            g[q, m, pl.ds(chunk_rows(k)[0] + hx, hz)] = res[m]
        give("cx0", k, 1, q, "xl")
        give("cp0", k, 1, q, "z+")
        give("cm0", k, 1, q, "z-")

    def f1a(k):
        got(("cx0", k))
        give("cxp0", k, 1, qrel(1, 0), "z+")
        give("cxm0", k, 1, qrel(1, 0), "z-")

    def f1b(k):
        s = sgn(k)
        got(("cp0" if s == 1 else "cm0", k))
        give("cf0", k, 1, qrel(0, -s), zdir[s])

    def f1c(k):
        u = -sgn(k)
        got(("cp1" if u == 1 else "cm1", k))
        give("cf1", k, 0, qrel(0, -u), zdir[u])
        give("cxa", k, 0, qrel(0, -u), "xl")

    def f1d(k):
        u = -sgn(k)
        got(("cm1" if u == 1 else "cp1", k))
        give("cxb", k, 0, qrel(0, u), "xl")

    def f2a(k):
        s = sgn(k)
        got(("cxp0" if s == 1 else "cxm0", k))
        give("cxf0", k, 1, qrel(1, -s), zdir[s])

    def f2b(k):
        got(("cf1", k))
        give("cxc", k, 0, qrel(0, 2), "xl")

    def gather_done(k):
        for name in LAST[sgn(k)]:
            got((name, k))

    def dd(block, start, size):
        rows = pl.ds(block * RB + start, size)

        def tile(n, carry):
            cols = pl.ds(pl.multiple_of(n * 256, 256), 256)
            dgate = jnp.concatenate([g[q, 1, rows] for q in range(8)], axis=1)
            dup = jnp.concatenate([g[q, 2, rows] for q in range(8)], axis=1)
            ds[block, pl.ds(start, size), cols] = (
                nt(dgate, wg[cols, :]) + nt(dup, wu[cols, :])
            ).astype(BF)
            return carry

        lax.fori_loop(0, 4, tile, 0)
        if start + size == RB:
            send(("sib", block), ds.at[block, pl.ds(HB, HB)], rsib.at[block], "co", "d")

    def chip_sum(block):
        k = POS[block]
        got(("sib", k))
        return f32(ds[k, pl.ds(0, HB)]) + f32(rsib[k])

    def forward(name, block, total, dst, to):
        rows = (POS[block], pl.ds(0, HB))
        ds[rows] = total.astype(BF)
        send(name, ds.at[rows], dst, to, "d")

    def d20():
        forward("c0", (2, 0), chip_sum((2, 0)), rc.at[0], "y+")

    def d21():
        forward("c1", (2, 1), chip_sum((2, 1)), rc.at[1], "y-")

    def dn0a():
        forward("rc", (-1, 0), chip_sum((-1, 0)), rd.at[1], "y-")

    def dn0b():
        total = chip_sum((1, 0))
        got("c0")
        forward("ra", (1, 0), total + f32(rc[0]), rd.at[0], "y+")

    def dn1():
        forward("rb", (1, 1), chip_sum((1, 1)), rd.at[2], "y+")

    def dn2():
        total = chip_sum((-1, 1))
        got("c1")
        forward("rd", (-1, 1), total + f32(rc[1]), rd.at[3], "y-")

    def d_other():
        total = chip_sum((0, 1))
        got("rb", "rd")
        forward("re", (0, 1), total + f32(rd[2]) + f32(rd[3]), rd.at[4], "x2")

    def d_final():
        total = chip_sum((0, 0))
        got("ra", "rc")
        total = total + f32(rd[0]) + f32(rd[1])
        got("re")
        gin_out[...] = (total + f32(rd[4])).astype(BF)

    wcopies = []

    def wtile(i, rows):
        m, n = i // 4, i % 4
        cols = pl.ds(n * 256, 256)
        pair = jnp.concatenate([g[2 * n, m, rows], g[2 * n + 1, m, rows]], axis=1)
        if m == 0:
            return (m, cols), tn(pair, xy[1, rows, :])
        return (m, slice(None), cols), tn(xy[0, rows, :], pair)

    def w1(i):
        at, value = wtile(i, pl.ds(0, FIRST))
        ws[at] = value.astype(BF)

    def w2(i):
        at, value = wtile(i, pl.ds(FIRST, EARLY - FIRST))
        ws[at] = (f32(ws[at]) + value).astype(BF)
        out(ws.at[at], part_out.at[at])

    def out(src, dst):
        copy = pltpu.make_async_copy(src, dst, lsem.at[5 + len(wcopies)])
        copy.start()
        wcopies.append(copy)

    def late_xy():
        out(xy.at[:, pl.ds(EARLY, LATE)], xyt_out)

    def late_g():
        out(g.at[:, :, pl.ds(EARLY, LATE)], gt_out)

    steps = {
        OWN: own, WTS: weights, INIT: init, A0: a0, A1: a1, A2: a2, A2A: a2a, A3: a3, A4: a4,
        A5: a5, A6: a6, A7: a7, MC: mc, M: mm, R1A: r1a, R1B: r1b, R2A: r2a, R2B: r2b,
        EA: ea, EB: eb, F1A: f1a, F1B: f1b, F1C: f1c, F1D: f1d, F2A: f2a, F2B: f2b,
        G: gather_done, D: dd, D20: d20, D21: d21, DN0A: dn0a, DN0B: dn0b, DN1: dn1,
        DN2: dn2, DX: d_other, DF: d_final, W1: w1, W2: w2, LX: late_xy, LG: late_g,
    }
    for step in SCHEDULE:
        steps[step[0]](*step[1:])

    wait_bytes(xy.at[:, pl.ds(0, 15 * HB)], ssem.at[groups["a"]])
    wait_bytes(xy.at[0, pl.ds(0, 15 * HB)], ssem.at[groups["d"]])
    for k in range(NC):
        wait_bytes(g.at[pl.ds(0, 7), :, pl.ds(0, 2 * CHUNKS[k][2])], ssem.at[groups[k]])
    for copy in wcopies:
        copy.wait()


(
    OWN, WTS, INIT, A0, A1, A2, A2A, A3, A4, A5, A6, A7, MC, M, R1A, R1B, R2A, R2B, EA, EB,
    F1A, F1B, F1C, F1D, F2A, F2B, G, D, D20, D21, DN0A, DN0B, DN1, DN2, DX, DF, W1, W2, LX, LG,
) = range(40)
SCHEDULE = (
    (OWN,), (INIT,), (A0,), (WTS,), (MC, 0), (M, 0), (R1A, 0), (A2A,), (MC, 1), (M, 1), (A2,),
    (A1,), (A3,), (R2B, 0), (MC, 2), (M, 2), (R1B, 0), (EB, 0), (R1A, 1), (MC, 3), (M, 3),
    (R1B, 1), (R1A, 2), (R2A, 0), (R1B, 2), (A4,), (F1B, 0), (F1A, 0), (A5,), (R2B, 1), (MC, 4),
    (R2A, 1), (M, 4), (R1A, 3), (R1B, 3), (EA, 0), (EB, 1), (R2A, 2), (R2B, 2), (A6,), (F2A, 0),
    (EA, 1), (A7,), (R1A, 4), (R1B, 4), (R2A, 3), (F1A, 1), (MC, 5), (M, 5), (F1D, 1), (F1C, 0),
    (F1B, 1), (EB, 2), (F1D, 0), (R2B, 3), (R2B, 4), (EA, 2), (F1C, 1), (EA, 3), (R2A, 4),
    (F2A, 1), (MC, 6), (M, 6), (R1B, 5), (R1A, 5), (F2B, 0), (F1A, 2), (F1B, 2), (F1D, 2),
    (F2B, 1), (EB, 3), (F1C, 2), (F1C, 3), (F1D, 3), (EB, 4), (EA, 4), (R1A, 6), (R2A, 5),
    (R1B, 6), (G, 0), (D, 7, 0, 80), (R2B, 5), (F2B, 2), (G, 1), (F1B, 3), (F2A, 2), (MC, 7),
    (M, 7), (F1A, 3), (F1C, 4), (F2B, 3), (R2B, 6), (F1B, 4), (F1A, 4), (EA, 5), (F1D, 4),
    (R2A, 6), (EB, 5), (G, 2), (D, 0, 0, 160), (R1A, 7), (R1B, 7), (F2A, 3), (MC, 8), (F2B, 4),
    (M, 8), (F2A, 4), (MC, 9), (F1C, 5), (M, 9), (F1D, 5), (F1B, 5), (EB, 6), (R2A, 7), (EA, 6),
    (F1A, 5), (G, 3), (D, 1, 0, 160), (R1A, 8), (R2B, 7), (R1B, 8), (R1B, 9), (G, 4),
    (D, 2, 0, 160), (F2B, 5), (EA, 7), (F1A, 6), (F1C, 6), (R1A, 9), (D20,), (F2A, 5), (MC, 10),
    (LX,), (M, 10), (F1D, 6), (R2A, 9), (F1B, 6), (EB, 7), (F1D, 7), (R2A, 8), (R2B, 8), (DN0B,),
    (F1C, 7), (F2B, 6), (R1B, 10), (F2A, 6), (G, 5), (D, 3, 0, 160), (R1A, 10), (R2B, 9), (EA, 9),
    (W1, 0), (F1A, 7), (D21,), (W1, 1), (EB, 8), (F1B, 7), (W1, 4), (W1, 2), (W1, 3), (W1, 8),
    (W1, 5), (R2B, 10), (W1, 6), (F1D, 9), (EA, 8), (EB, 9), (W1, 10), (F2B, 7), (F2A, 7),
    (F1A, 8), (R2A, 10), (W1, 7), (W1, 11), (EB, 10), (W1, 9), (G, 6), (D, 4, 0, 160), (F1C, 9),
    (F1A, 9), (F1B, 9), (F1C, 8), (F1B, 8), (F1D, 8), (DN1,), (G, 7), (D, 5, 0, 160), (F2A, 8),
    (EA, 10), (F2A, 9), (F1A, 10), (F1B, 10), (DN2,), (F2B, 9), (F2B, 8), (F1C, 10), (F1D, 10),
    (G, 9), (F2A, 10), (G, 8), (D, 6, 0, 160), (F2B, 10), (W2, 4), (DX,), (W2, 0), (DN0A,),
    (W2, 1), (W2, 2), (W2, 3), (G, 10), (LG,), (D, 7, 80, 80), (W2, 5), (W2, 6), (W2, 7), (W2, 8),
    (W2, 11), (W2, 9), (W2, 10), (DF,),
)


def finish(gin, part, xyt, gt):
    def body(gin, part, xt, yt, gta, gtd, gin_out, gate_out, up_out, down_out):
        gin_out[...] = gin[...]
        for m, out in ((1, gate_out), (2, up_out)):
            rhs = jnp.concatenate([gta[q, m] for q in range(8)], axis=1)
            out[...] = (f32(part[m]) + tn(xt[0], rhs)).astype(BF)
        lhs = jnp.concatenate([gtd[q, 0] for q in range(gtd.shape[0])], axis=1)
        down_out[...] = (f32(part[0]) + tn(lhs, yt[0])).astype(BF)

    whole = jax.ShapeDtypeStruct((W, W), BF)
    rows = W // FSTEPS
    tile = pl.BlockSpec((rows, W), lambda i: (i, 0))
    gin_tile = pl.BlockSpec((HB, W // FSTEPS), lambda i: (0, i))
    return pl.pallas_call(
        body,
        name="finish_weight_grads",
        grid=(FSTEPS,),
        out_shape=(jax.ShapeDtypeStruct((HB, W), BF), whole, whole, whole),
        in_specs=[
            gin_tile,
            pl.BlockSpec((3, rows, W), lambda i: (0, i, 0)),
            pl.BlockSpec((1, LATE, rows), lambda i: (0, 0, i)),
            pl.BlockSpec((1, LATE, W), lambda i: (1, 0, 0)),
            pl.BlockSpec((8, 3, LATE, 128), lambda i: (0, 0, 0, 0)),
            pl.BlockSpec((8 // FSTEPS, 1, LATE, 128), lambda i: (i, 0, 0, 0)),
        ],
        out_specs=(gin_tile, tile, tile, tile),
        compiler_params=pltpu.CompilerParams(vmem_limit_bytes=FVMEM * 2**20),
    )(gin, part, xyt, xyt, gt, gt)


def exchange(inputs, grad_out, w_gate, w_up, w_down):
    def vmem(*shape, dtype=BF):
        return pltpu.VMEM(shape, dtype)

    def chunk_scratch(k):
        hx, hz = chunk_split(k)
        return (
            vmem(2, 4, 3, hx, 128), vmem(4, 2, 3, hz, 128), vmem(4, 3, hx, 128),
            vmem(3, hx, 128), vmem(3, hx, 128), vmem(3, hx, 128),
            vmem(2, 3, hz, 128), vmem(2, 3, hz, 128), vmem(2, 3, hz, 128),
            vmem(3, hz, 128),
        )

    scratch = [
        vmem(2, TOKENS, W), vmem(W, W), vmem(W, W), vmem(W, W),
        [chunk_scratch(k) for k in range(NC)],
        vmem(8, 3, TOKENS, 128),
        vmem(NB, RB, W), vmem(NB, HB, W), vmem(2, HB, W), vmem(5, HB, W),
        vmem(3, W, W),
        pltpu.SemaphoreType.DMA((NSEND,)), pltpu.SemaphoreType.DMA((NRECV,)),
        pltpu.SemaphoreType.DMA((19,)),
    ]
    anywhere = pl.BlockSpec(memory_space=pl.ANY)
    return pl.pallas_call(
        kernel,
        name="exchange",
        out_shape=(
            jax.ShapeDtypeStruct((HB, W), BF),
            jax.ShapeDtypeStruct((3, W, W), BF),
            jax.ShapeDtypeStruct((2, LATE, W), BF),
            jax.ShapeDtypeStruct((8, 3, LATE, 128), BF),
        ),
        in_specs=[anywhere] * 5,
        out_specs=(pl.BlockSpec(memory_space=pltpu.VMEM), anywhere, anywhere, anywhere),
        scratch_shapes=scratch,
        compiler_params=pltpu.CompilerParams(
            collective_id=0, has_side_effects=True, vmem_limit_bytes=EVMEM * 2**20
        ),
    )(inputs, grad_out, w_gate, w_up, w_down)


def shards(inputs, grad_out, w_gate, w_up, w_down):
    grad_in, part, xyt, gt = exchange(inputs, grad_out, w_gate, w_up, w_down)
    return finish(grad_in, part, xyt, gt)


def solution(mesh):
    return jax.shard_map(
        shards,
        mesh=mesh,
        in_specs=(
            P(("row", "dep"), "col"),
            P(("row", "dep"), "col"),
            P("col", ("row", "dep")),
            P("col", ("row", "dep")),
            P(("row", "dep"), "col"),
        ),
        out_specs=(
            P(("row", "dep"), "col"),
            P("col", ("row", "dep")),
            P("col", ("row", "dep")),
            P(("row", "dep"), "col"),
        ),
        check_vma=False,
    )
```
